768 devices in a mesh: dp: 8 (over y_hi, core), ctx: 8 (over y_lo, x), tp: 12 (over z).
Axes of the slice: x: 4, y: 8 (y_hi: 4, y_lo: 2; y = y_hi * 2 + y_lo), z: 12, core: 2. Of those that a mesh axis runs over, the one named last changes fastest.
Arguments:
- grad_out: bfloat16 [64, 24, 4096], P(('dp', 'ctx'), 'tp'), may hold values from -6 to 6
- probs: bfloat16 [64, 24, 8], P(('dp', 'ctx')), may hold values from 0.099609375 to 1
- expert_ids: int32 [64, 24, 8], P(('dp', 'ctx')), may hold values from 0 to 63, all different within a row; in each aligned block of 24 rows (0 to 23, 24 to 47, ..., all dimensions but the last counted through in order) at most 4 rows name the same one
- saved_inputs: bfloat16 [64, 64, 4, 4096], P(('dp', 'ctx')), may hold values from -6 to 6
- w_gate: bfloat16 [64, 4096, 768], P(('dp', 'ctx'), None, 'tp'), may hold values from -0.09375 to 0.09375
- w_up: bfloat16 [64, 4096, 768], P(('dp', 'ctx'), None, 'tp'), may hold values from -0.09375 to 0.09375
- w_down: bfloat16 [64, 768, 4096], P(('dp', 'ctx'), 'tp'), may hold values from -0.046875 to 0.046875
Outputs:
- grad_tokens: bfloat16 [64, 24, 4096], P(('dp', 'ctx'), 'tp')
- grad_probs: float32 [64, 24, 8], P(('dp', 'ctx'), 'tp')
- grad_gate: bfloat16 [64, 4096, 768], P(('dp', 'ctx'), None, 'tp')
- grad_up: bfloat16 [64, 4096, 768], P(('dp', 'ctx'), None, 'tp')
- grad_down: bfloat16 [64, 768, 4096], P(('dp', 'ctx'), 'tp')
The draws below stay inside these ranges and needn't reach their ends.
Inputs may be any that keep to these rules, and one draw needn't show every extreme that they name: `expert_ids`: each row names 8 different experts. Within one index of the first dimension no expert is named by more than 4 rows, a bound that some block reaches.
All inputs are finite; a program needn't handle non-finite values.
Results may differ from the reference program's by a relative error of at most 0.0065.
Values may be sent and summed in bfloat16 or wider, within the bound.
No kernel may reach another device: no remote copies, remote signals or barrier semaphores. Data moves between devices by JAX's collectives and lax.ppermute only.
A program may use at most 32 MiB of HBM per device.

```python
import math
import jax
import jax.numpy as jnp
import numpy as np
from jax import lax

D = 4096
HIDDEN_SIZE = 768
TOPK = 8
EXPERTS = 64
GROUPS = 64
GROUP_TOK = 24
CAP = 4
N_TP = 12


def block_levels(key, extent, cuts, smallest, high):
    factor_of, own = 1.0, jax.random.fold_in(key, 6)
    for position, blocks in cuts:
        draws = jnp.exp(jax.random.uniform(jax.random.fold_in(own, position), (blocks,), jnp.float32, smallest / len(cuts), high / len(cuts)))
        factor_of = factor_of * jnp.repeat(draws, extent[position] // blocks).reshape([-1 if axis == position else 1 for axis in range(len(extent))])
    return factor_of


def shared_out(stream_key, own, number, rows, amount, top, reach, slope):
    order = jax.random.permutation(stream_key, amount)
    packed, usual = portions_of(amount, rows * top, reach, slope, True), portions_of(amount, rows * top, reach, slope, False)
    places = jnp.arange(amount)

    def named(tallies, turn):
        used = int((tallies > 0).sum())
        fixed = max(1, used // 4)
        moved = fixed + (places - fixed + turn * (used - fixed)) % max(1, amount - fixed)
        return jnp.zeros((amount,), jnp.int32).at[order[jnp.where(places < fixed, places, moved)]].set(jnp.asarray(tallies, jnp.int32))

    tallies = jnp.where(number % 4 == 0, named(packed, number // 4), named(usual, number - number // 4 - 1))
    mixed = jax.random.permutation(jax.random.fold_in(own, 3), amount)
    donor, sink = mixed[0:amount // 2 * 2:2], mixed[1:amount // 2 * 2:2]
    room = jnp.minimum(tallies[donor] - 1, reach - tallies[sink]) // 2
    room = jnp.where((donor == order[0]) | (sink == order[0]) | (tallies[sink] == 0), 0, jnp.maximum(room, 0))
    moved = jax.random.randint(jax.random.fold_in(own, 4), (amount // 2,), 0, 1 << 20) % (room + 1)
    tallies = tallies.at[donor].add(-moved).at[sink].add(moved)
    members = jnp.searchsorted(jnp.cumsum(tallies), jnp.arange(rows * top), side="right").astype(jnp.int32)
    table = members.reshape(top, rows).T
    table = table[jax.random.permutation(jax.random.fold_in(own, 1), rows)]
    turn = jax.random.randint(jax.random.fold_in(own, 2), (rows, 1), 0, top)
    return jnp.take_along_axis(table, (jnp.arange(top)[None, :] + turn) % top, axis=1)


def portions_of(count, total, bound, lean, full):
    portions = [(1 << 20) // math.isqrt(standing ** lean) + 1 for standing in range(1, count + 1)]
    largest = bound if full else min(bound, max(-(-total // count), total * portions[0] // sum(portions)))
    least = 1 if total - largest >= count - 1 else 0
    counts, surplus = [largest] + [least] * (count - 1), total - largest - least * (count - 1)
    while surplus > 0:
        movable = [i for i in range(1, count) if counts[i] < largest] or [i for i in range(1, count) if counts[i] < bound]
        mass, remaining = sum([portions[i] for i in movable]), surplus
        for i in movable:
            addition = min(bound - counts[i], max(1, remaining * portions[i] // mass), surplus)
            counts[i] = counts[i] + addition
            surplus = surplus - addition
    return np.array(counts)


def bell_draw(stream_key, extent, width, bound, pieces=(), held_as=jnp.bfloat16):
    level = block_levels(stream_key, extent, pieces, -0.22, 0.18) if pieces else 1.0
    values = jax.random.normal(stream_key, extent, jnp.float32) * width * level
    return jnp.minimum(jnp.maximum(values, -bound), bound).astype(held_as)


def setup_inputs(seed: int = 0) -> dict:
    seeds = jax.random.split(jax.random.key(seed), 8)
    grad_out = bell_draw(seeds[0], (GROUPS, GROUP_TOK, D), 1.0, 6.0, ((0, 64), (1, 12)))
    probs = jnp.clip(jnp.exp(math.log(1.0) - 2.306499 * jax.random.uniform(seeds[1], (GROUPS, GROUP_TOK, TOPK), jnp.float32) ** block_levels(seeds[1], (GROUPS, GROUP_TOK, TOPK), ((0, 64),), -0.2, 0.2)), 0.099609375, 1.0).astype(jnp.bfloat16)
    expert_ids_keys = jax.random.split(jax.random.fold_in(seeds[2], 1), GROUPS * GROUP_TOK // GROUP_TOK)
    expert_ids_turns = jax.random.permutation(jax.random.fold_in(seeds[2], 3), GROUPS * GROUP_TOK // GROUP_TOK)
    expert_ids = jax.vmap(lambda own, number: shared_out(jax.random.fold_in(seeds[2], 2), own, number, GROUP_TOK, EXPERTS, TOPK, CAP, 2))(expert_ids_keys, expert_ids_turns).reshape((GROUPS, GROUP_TOK, TOPK))
    saved_inputs = bell_draw(seeds[3], (EXPERTS, GROUPS, CAP, D), 1.0, 6.0, ((0, 64),))
    w_gate = bell_draw(seeds[4], (EXPERTS, D, HIDDEN_SIZE), D ** -0.5, 0.09375, ((0, 64), (2, 12)))
    w_up = bell_draw(seeds[5], (EXPERTS, D, HIDDEN_SIZE), D ** -0.5, 0.09375, ((0, 64), (2, 12)))
    w_down = bell_draw(seeds[6], (EXPERTS, HIDDEN_SIZE, D), (4 * D) ** -0.5, 0.046875, ((0, 64), (1, 12)))
    return dict(grad_out=grad_out, probs=probs, expert_ids=expert_ids, saved_inputs=saved_inputs, w_gate=w_gate, w_up=w_up, w_down=w_down)


def slot_index(routes, experts, capacity):
    flattened = routes.reshape(-1)
    onehot = (flattened[:, None] == jnp.arange(experts, dtype=jnp.int32)[None, :]).astype(jnp.int32)
    before = jnp.cumsum(onehot, axis=0) - onehot
    ranking = jnp.sum(before * onehot, axis=1)
    return (flattened * capacity + ranking).reshape(routes.shape).astype(jnp.int32)


def chooser_table(slots, slot_count):
    return (slots[None, :, :] == jnp.arange(slot_count, dtype=jnp.int32)[:, None, None]).astype(jnp.float32)


def expert_terms(rows_input, rows_grad, rows_weight, gate_slice, up_slice, down_slice):
    gate_pre = jnp.dot(rows_input, gate_slice, preferred_element_type=jnp.float32)
    up_pre = jnp.dot(rows_input, up_slice, preferred_element_type=jnp.float32)
    sigmoid_gate = jax.nn.sigmoid(gate_pre)
    activated = gate_pre * sigmoid_gate
    hidden = activated * up_pre
    upward = lax.dot_general(rows_grad, down_slice, (((1,), (1,)), ((), ())), preferred_element_type=jnp.float32)
    part_prob = jnp.sum(hidden * upward, axis=1).astype(jnp.bfloat16)
    weight_col = rows_weight.astype(jnp.float32)[:, None]
    hidden_grad = weight_col * upward
    gate_grad = (hidden_grad * up_pre * sigmoid_gate * (1.0 + gate_pre * (1.0 - sigmoid_gate))).astype(jnp.bfloat16)
    up_grad = (hidden_grad * activated).astype(jnp.bfloat16)
    part_grad = lax.dot_general(gate_grad, gate_slice, (((1,), (1,)), ((), ())), preferred_element_type=jnp.float32)
    part_grad = part_grad + lax.dot_general(up_grad, up_slice, (((1,), (1,)), ((), ())), preferred_element_type=jnp.float32)
    part_grad = part_grad.astype(jnp.bfloat16)
    scaled = (weight_col * rows_grad.astype(jnp.float32)).astype(jnp.bfloat16)
    grad_down = lax.dot_general(hidden.astype(jnp.bfloat16), scaled, (((0,), (0,)), ((), ())), preferred_element_type=jnp.float32).astype(jnp.bfloat16)
    grad_gate = lax.dot_general(rows_input, gate_grad, (((0,), (0,)), ((), ())), preferred_element_type=jnp.float32).astype(jnp.bfloat16)
    grad_up = lax.dot_general(rows_input, up_grad, (((0,), (0,)), ((), ())), preferred_element_type=jnp.float32).astype(jnp.bfloat16)
    return part_grad, part_prob, grad_gate, grad_up, grad_down


def reference(grad_out, probs, expert_ids, saved_inputs, w_gate, w_up, w_down):
    slot_count = EXPERTS * CAP
    chooser = jax.vmap(lambda routes: chooser_table(slot_index(routes, EXPERTS, CAP), slot_count))(expert_ids)
    picker = jnp.sum(chooser, axis=3)
    highest = lax.Precision.HIGHEST
    sent_grad = jnp.einsum('gsj,gjd->gsd', picker, grad_out.astype(jnp.float32), precision=highest).astype(jnp.bfloat16)
    sent_weight = jnp.einsum('gsjk,gjk->gs', chooser, probs.astype(jnp.float32), precision=highest).astype(jnp.bfloat16)
    grad_rows = sent_grad.reshape(GROUPS, EXPERTS, CAP, D).transpose(1, 0, 2, 3).reshape(EXPERTS, GROUPS * CAP, D)
    weight_rows = sent_weight.reshape(GROUPS, EXPERTS, CAP).transpose(1, 0, 2).reshape(EXPERTS, GROUPS * CAP)
    input_rows = saved_inputs.reshape(EXPERTS, GROUPS * CAP, D)
    width_slice = HIDDEN_SIZE // N_TP

    def one_expert(items):
        rows_input, rows_grad, rows_weight, gate_full, up_full, down_full = items
        grad_total = jnp.zeros((GROUPS * CAP, D), jnp.float32)
        prob_total = jnp.zeros((GROUPS * CAP,), jnp.float32)
        gate_parts, up_parts, down_parts = [], [], []
        for piece_index in range(N_TP):
            lower = piece_index * width_slice
            upper = lower + width_slice
            part_grad, part_prob, grad_gate, grad_up, grad_down = expert_terms(
                rows_input, rows_grad, rows_weight, gate_full[:, lower:upper], up_full[:, lower:upper], down_full[lower:upper, :])
            grad_total = grad_total + part_grad.astype(jnp.float32)
            prob_total = prob_total + part_prob.astype(jnp.float32)
            gate_parts.append(grad_gate)
            up_parts.append(grad_up)
            down_parts.append(grad_down)
        return grad_total, prob_total, jnp.concatenate(gate_parts, axis=1), jnp.concatenate(up_parts, axis=1), jnp.concatenate(down_parts, axis=0)

    grad_total, prob_total, grad_gate, grad_up, grad_down = lax.map(
        one_expert, (input_rows, grad_rows, weight_rows, w_gate, w_up, w_down))
    back_grad = grad_total.reshape(EXPERTS, GROUPS, CAP, D).transpose(1, 0, 2, 3).reshape(GROUPS, slot_count, D)
    back_prob = prob_total.reshape(EXPERTS, GROUPS, CAP).transpose(1, 0, 2).reshape(GROUPS, slot_count)
    grad_tokens = jnp.einsum('gsj,gsd->gjd', picker, back_grad, precision=highest).astype(jnp.bfloat16)
    grad_probs = jnp.einsum('gsjk,gs->gjk', chooser, back_prob, precision=highest)
    return grad_tokens, grad_probs, grad_gate, grad_up, grad_down
```

```python
import jax
import jax.numpy as jnp
from jax import lax
from jax.experimental import pallas as pl
from jax.experimental.pallas import tpu as pltpu
from jax.sharding import PartitionSpec as P

PARTS = 3
LANES = 128
F32, BF16 = jnp.float32, jnp.bfloat16
COLUMN = ("dp", "ctx")
VMEM = pl.BlockSpec(memory_space=pltpu.VMEM)
SMEM = pl.BlockSpec(memory_space=pltpu.SMEM)


def call(kernel, outs, in_specs, flops, bytes_accessed, scratch=()):
    return pl.pallas_call(
        kernel,
        out_shape=outs,
        in_specs=in_specs,
        out_specs=jax.tree.map(lambda _: VMEM, outs),
        scratch_shapes=scratch,
        compiler_params=pltpu.CompilerParams(vmem_limit_bytes=40 << 20),
        cost_estimate=pl.CostEstimate(
            flops=flops, bytes_accessed=bytes_accessed, transcendentals=0
        ),
    )


def route_kernel(cap, ids_ref, probs_ref, pick_ref, back_ref):
    top, tokens = ids_ref.shape
    slots, width = pick_ref.shape
    row = lax.broadcasted_iota(jnp.int32, (slots, tokens), 0)
    expert, place = row // cap, row % cap
    ids = ids_ref[...]
    probs = probs_ref[...].astype(F32)
    member = jnp.zeros((slots, tokens), F32)
    weight = jnp.zeros((slots, tokens), F32)
    for k in range(top):
        same = expert == ids[k : k + 1, :]
        member = jnp.where(same, 1.0, member)
        weight = jnp.where(same, probs[k : k + 1, :], weight)
    before = lax.broadcasted_iota(jnp.int32, (tokens, tokens), 0) < lax.broadcasted_iota(
        jnp.int32, (tokens, tokens), 1
    )
    rank = jnp.dot(
        member.astype(BF16), before.astype(F32).astype(BF16), preferred_element_type=F32
    )
    pick = jnp.where(rank == place.astype(F32), member, 0.0)
    slot_weight = jnp.sum(pick * weight, axis=1, keepdims=True)
    tail = lax.broadcasted_iota(jnp.int32, (slots, width - tokens), 1)
    full = jnp.concatenate([pick, jnp.where(tail == 0, slot_weight, 0.0)], axis=1)
    pick_ref[...] = full.astype(BF16)
    back_ref[...] = full.T.astype(BF16)


def send_kernel(part_ref, pick_ref, column_ref, out_ref):
    peers, own, width = column_ref.shape
    tokens = peers * own
    experts, cap, _ = out_ref.shape
    column = column_ref[...].astype(F32).reshape(tokens, width)
    rest = pick_ref.shape[1] - tokens
    lane = lax.broadcasted_iota(jnp.int32, (rest, width), 1)
    deep = lax.broadcasted_iota(jnp.int32, (rest, width), 0)
    padded = (deep == 0) & (lane >= width - LANES) & (part_ref[0] == PARTS - 1)
    column = jnp.concatenate([column, padded.astype(F32)], axis=0).astype(BF16)
    rows = jnp.dot(pick_ref[...], column, preferred_element_type=F32)
    out_ref[...] = rows.reshape(experts, cap, width).astype(BF16)


def expert_kernel(
    part_ref, mine_ref, low_ref, high_ref, gate_ref, up_ref, w_gate_ref, w_up_ref, w_down_ref,
    own_ref, to_high_ref, to_low_ref, rows_ref, gate_grad_ref, up_grad_ref, hidden_ref,
    stage_ref,
):
    experts, cap, width = mine_ref.shape
    slots = experts * cap
    model = w_down_ref.shape[1]
    part = part_ref[0]
    above, below = lax.rem(part + 1, PARTS), lax.rem(part + PARTS - 1, PARTS)
    for ref, place in ((mine_ref, part), (low_ref, below), (high_ref, above)):
        rows_ref[:, pl.ds(pl.multiple_of(place * width, LANES), width)] = ref[...].reshape(
            slots, width
        )
    nt = (((1,), (1,)), ((), ()))
    upward = lax.dot_general(
        rows_ref[:, :model], w_down_ref[...], nt, preferred_element_type=F32
    )
    weight = rows_ref[:, model : model + LANES].astype(F32)[:, :1]
    gate_pre, up_pre = gate_ref[...], up_ref[...]
    sigmoid = jax.nn.sigmoid(gate_pre)
    activated = gate_pre * sigmoid
    hidden = activated * up_pre
    part_prob = jnp.sum(hidden * upward, axis=1, keepdims=True)
    hidden_grad = weight * upward
    gate_grad = (hidden_grad * up_pre * sigmoid * (1.0 + gate_pre * (1.0 - sigmoid))).astype(BF16)
    up_grad = (hidden_grad * activated).astype(BF16)
    gate_grad_ref[...] = gate_grad
    up_grad_ref[...] = up_grad
    hidden_ref[...] = (hidden * weight).astype(BF16)
    grads = jnp.dot(gate_grad, w_gate_ref[...], preferred_element_type=F32)
    grads = grads + jnp.dot(up_grad, w_up_ref[...], preferred_element_type=F32)
    stage_ref[:, :model] = grads.astype(BF16)
    stage_ref[:, model:] = jnp.broadcast_to(
        part_prob, (slots, PARTS * width - model)
    ).astype(BF16)
    for ref, place in ((own_ref, part), (to_high_ref, above), (to_low_ref, below)):
        ref[...] = stage_ref[:, pl.ds(pl.multiple_of(place * width, LANES), width)]


def sum_kernel(own_ref, low_ref, high_ref, out_ref):
    total = own_ref[...].astype(F32) + low_ref[...].astype(F32) + high_ref[...].astype(F32)
    out_ref[...] = total.reshape(out_ref.shape).astype(BF16)


def combine_kernel(cap, part_ref, back_ref, ids_ref, got_ref, out_ref):
    peers, own, width = out_ref.shape
    tokens = peers * own
    experts, _, _ = got_ref.shape
    slots = experts * cap
    got = got_ref[...].astype(F32).reshape(slots, width)
    back = back_ref[...]
    sums = jnp.dot(back, got.astype(BF16), preferred_element_type=F32)[:tokens]
    prob = got[:, width - LANES :].T[:1, :]
    picked = back[:tokens].astype(F32) * prob
    expert = lax.broadcasted_iota(jnp.int32, (tokens, slots), 1) // cap
    ids = ids_ref[...]
    lane = lax.broadcasted_iota(jnp.int32, (tokens, LANES), 1)
    by_choice = jnp.zeros((tokens, LANES), F32)
    for k in range(ids.shape[1]):
        one = jnp.sum(
            jnp.where(expert == ids[:, k : k + 1], picked, 0.0), axis=1, keepdims=True
        )
        by_choice = jnp.where(lane == k, one, by_choice)
    last = jnp.where(part_ref[0] == PARTS - 1, by_choice, sums[:, width - LANES :])
    sums = jnp.concatenate([sums[:, : width - LANES], last], axis=1)
    out_ref[...] = sums.reshape(peers, own, width)


def finish_kernel(got_ref, tokens_ref, probs_ref):
    peers, _, width = got_ref.shape
    model = tokens_ref.shape[1]
    for part in range(PARTS):
        total = got_ref[part]
        for peer in range(part + PARTS, peers, PARTS):
            total = total + got_ref[peer]
        low = part * width
        high = min(low + width, model)
        tokens_ref[:, low:high] = total[:, : high - low].astype(BF16)
        if part == PARTS - 1:
            probs_ref[...] = total[:, width - LANES : width - LANES + probs_ref.shape[1]]


def body(grad_out, probs, expert_ids, saved_inputs, w_gate, w_up, w_down):
    tp_count = lax.axis_size("tp")
    experts, cap, model = saved_inputs.shape[1:]
    slots = experts * cap
    own, top = grad_out.shape[1], expert_ids.shape[2]
    tokens = tp_count * own
    width = -(-(model + LANES) // (PARTS * LANES)) * LANES
    units = w_down.shape[1]
    wide = tokens + 8
    part = lax.rem(lax.axis_index("tp"), PARTS).astype(jnp.int32).reshape(1)
    rise = [(i, (i + 1) % tp_count) for i in range(tp_count)]
    fall = [(i, (i - 1) % tp_count) for i in range(tp_count)]

    padded = jnp.pad(grad_out[0], ((0, 0), (0, PARTS * width - model)))
    thirds = padded.reshape(own, PARTS, width).transpose(1, 0, 2)
    column = lax.all_to_all(
        jnp.tile(thirds, (tp_count // PARTS, 1, 1)), "tp", split_axis=0, concat_axis=0, tiled=True
    )
    ids = expert_ids[0]
    pick, back = call(
        lambda *refs: route_kernel(cap, *refs),
        [
            jax.ShapeDtypeStruct((slots, wide), BF16),
            jax.ShapeDtypeStruct((wide, slots), BF16),
        ],
        [VMEM] * 2,
        1000000,
        100000,
    )(ids.T, probs[0].T)
    sent = call(
        send_kernel,
        jax.ShapeDtypeStruct((experts, cap, width), BF16),
        [SMEM, VMEM, VMEM],
        2 * slots * wide * width,
        2 * slots * width,
    )(part, pick, column)
    mine = lax.all_to_all(sent, COLUMN, split_axis=0, concat_axis=0, tiled=True)
    low = lax.ppermute(mine, "tp", rise)
    high = lax.ppermute(mine, "tp", fall)

    rows_input = saved_inputs[0].reshape(slots, model)
    gate_pre = jnp.dot(rows_input, w_gate[0], preferred_element_type=F32)
    up_pre = jnp.dot(rows_input, w_up[0], preferred_element_type=F32)
    slab = jax.ShapeDtypeStruct((slots, width), BF16)
    thin = jax.ShapeDtypeStruct((slots, units), BF16)
    mine_grad, to_high, to_low, rows, gate_grad, up_grad, hidden = call(
        expert_kernel,
        [slab, slab, slab, jax.ShapeDtypeStruct((slots, PARTS * width), BF16), thin, thin, thin],
        [SMEM] + [VMEM] * 8,
        6 * slots * model * units,
        12 * slots * model,
        (pltpu.VMEM((slots, PARTS * width), BF16),),
    )(part, mine, low, high, gate_pre, up_pre, w_gate[0].T, w_up[0].T, w_down[0])
    from_low = lax.ppermute(to_high, "tp", rise)
    from_high = lax.ppermute(to_low, "tp", fall)

    tn = (((0,), (0,)), ((), ()))
    grad_gate = lax.dot_general(rows_input, gate_grad, tn, preferred_element_type=F32)
    grad_up = lax.dot_general(rows_input, up_grad, tn, preferred_element_type=F32)
    grad_down = lax.dot_general(hidden, rows[:, :model], tn, preferred_element_type=F32)

    summed = call(
        sum_kernel,
        jax.ShapeDtypeStruct((experts, cap, width), BF16),
        [VMEM] * 3,
        3 * slots * width,
        8 * slots * width,
    )(mine_grad, from_low, from_high)
    got = lax.all_to_all(summed, COLUMN, split_axis=0, concat_axis=0, tiled=True)
    combined = call(
        lambda *refs: combine_kernel(cap, *refs),
        jax.ShapeDtypeStruct((tp_count, own, width), F32),
        [SMEM] + [VMEM] * 3,
        2 * slots * wide * width,
        2 * slots * width,
    )(part, back, ids, got)
    last = lax.all_to_all(combined, "tp", split_axis=0, concat_axis=0, tiled=True)
    grad_tokens, grad_probs = call(
        finish_kernel,
        [
            jax.ShapeDtypeStruct((own, model), BF16),
            jax.ShapeDtypeStruct((own, top), F32),
        ],
        [VMEM],
        1000,
        4 * tokens * width,
    )(last)
    return (
        grad_tokens[None],
        grad_probs[None],
        grad_gate.astype(BF16)[None],
        grad_up.astype(BF16)[None],
        grad_down.astype(BF16)[None],
    )


def solution(mesh):
    placed = (
        P(COLUMN, "tp", None),
        P(COLUMN, None, None),
        P(COLUMN, None, None),
        P(COLUMN, None, None, None),
        P(COLUMN, None, "tp"),
        P(COLUMN, None, "tp"),
        P(COLUMN, "tp", None),
    )
    return jax.shard_map(
        body,
        mesh=mesh,
        in_specs=placed,
        out_specs=(
            P(COLUMN, "tp", None),
            P(COLUMN, "tp", None),
            P(COLUMN, None, "tp"),
            P(COLUMN, None, "tp"),
            P(COLUMN, "tp", None),
        ),
        check_vma=False,
    )
```

```python
import jax
import jax.numpy as jnp
from jax import lax
from jax.experimental import pallas as pl
from jax.experimental.pallas import tpu as pltpu
from jax.sharding import PartitionSpec as P

PARTS = 3
LANES = 128
F32, BF16 = jnp.float32, jnp.bfloat16
COLUMN = ("dp", "ctx")
VMEM = pl.BlockSpec(memory_space=pltpu.VMEM)
SMEM = pl.BlockSpec(memory_space=pltpu.SMEM)


def call(kernel, outs, in_specs, flops, bytes_accessed, scratch=()):
    return pl.pallas_call(
        kernel,
        out_shape=outs,
        in_specs=in_specs,
        out_specs=jax.tree.map(lambda _: VMEM, outs),
        scratch_shapes=scratch,
        compiler_params=pltpu.CompilerParams(vmem_limit_bytes=16 << 20),
        cost_estimate=pl.CostEstimate(
            flops=flops, bytes_accessed=bytes_accessed, transcendentals=0
        ),
    )


def route_kernel(cap, ids_ref, probs_ref, pick_ref, back_ref):
    top, tokens = ids_ref.shape
    slots, width = pick_ref.shape
    row = lax.broadcasted_iota(jnp.int32, (slots, tokens), 0)
    expert, place = row // cap, row % cap
    ids = ids_ref[...]
    probs = probs_ref[...].astype(F32)
    member = jnp.zeros((slots, tokens), F32)
    weight = jnp.zeros((slots, tokens), F32)
    for k in range(top):
        same = expert == ids[k : k + 1, :]
        member = jnp.where(same, 1.0, member)
        weight = jnp.where(same, probs[k : k + 1, :], weight)
    before = lax.broadcasted_iota(jnp.int32, (tokens, tokens), 0) < lax.broadcasted_iota(
        jnp.int32, (tokens, tokens), 1
    )
    rank = jnp.dot(
        member.astype(BF16), before.astype(F32).astype(BF16), preferred_element_type=F32
    )
    pick = jnp.where(rank == place.astype(F32), member, 0.0)
    slot_weight = jnp.sum(pick * weight, axis=1, keepdims=True)
    tail = lax.broadcasted_iota(jnp.int32, (slots, width - tokens), 1)
    full = jnp.concatenate([pick, jnp.where(tail == 0, slot_weight, 0.0)], axis=1)
    pick_ref[...] = full.astype(BF16)
    back_ref[...] = full.T.astype(BF16)


def thirds_kernel(grad_ref, out_ref):
    peers, _, width = out_ref.shape
    model = grad_ref.shape[1]
    for part in range(PARTS):
        piece = grad_ref[:, part * width : min(part * width + width, model)]
        if piece.shape[1] < width:
            piece = jnp.concatenate(
                [piece, jnp.zeros((piece.shape[0], width - piece.shape[1]), BF16)], axis=1
            )
        for peer in range(part, peers, PARTS):
            out_ref[peer] = piece


def weights_kernel(part_ref, gate_ref, up_ref, down_ref, own_ref, high_ref, low_ref, stage_ref):
    units, model = gate_ref.shape
    width = own_ref.shape[1]
    part = part_ref[0]
    above, below = lax.rem(part + 1, PARTS), lax.rem(part + PARTS - 1, PARTS)
    for at, ref in enumerate((gate_ref, up_ref, down_ref)):
        stage_ref[at * units : (at + 1) * units, :model] = ref[...]
    stage_ref[:, model:] = jnp.zeros((PARTS * units, PARTS * width - model), BF16)
    for ref, place in ((own_ref, part), (high_ref, above), (low_ref, below)):
        ref[...] = stage_ref[:, pl.ds(pl.multiple_of(place * width, LANES), width)]


def send_kernel(part_ref, pick_ref, column_ref, out_ref):
    peers, own, width = column_ref.shape
    tokens = peers * own
    experts, cap, _ = out_ref.shape
    column = column_ref[...].astype(F32).reshape(tokens, width)
    rest = pick_ref.shape[1] - tokens
    lane = lax.broadcasted_iota(jnp.int32, (rest, width), 1)
    deep = lax.broadcasted_iota(jnp.int32, (rest, width), 0)
    padded = (deep == 0) & (lane >= width - LANES) & (part_ref[0] == PARTS - 1)
    column = jnp.concatenate([column, padded.astype(F32)], axis=0).astype(BF16)
    rows = jnp.dot(pick_ref[...], column, preferred_element_type=F32)
    out_ref[...] = rows.reshape(experts, cap, width).astype(BF16)


def upward_kernel(part_ref, got_ref, own_w_ref, low_w_ref, high_w_ref, rows_ref, own_ref, to_low_ref, to_high_ref):
    experts, cap, width = got_ref.shape
    slots, units = experts * cap, own_w_ref.shape[0] // 3
    rows = got_ref[...].reshape(slots, width)
    rows_ref[...] = rows
    nt = (((1,), (1,)), ((), ()))
    weight = jnp.where(
        part_ref[0] == PARTS - 1, rows[:, width - LANES : width - LANES + units].astype(F32), 0.0
    )
    for w_ref, ref in ((own_w_ref, own_ref), (low_w_ref, to_low_ref), (high_w_ref, to_high_ref)):
        product = lax.dot_general(rows, w_ref[2 * units :], nt, preferred_element_type=F32)
        ref[...] = jnp.concatenate([product, weight], axis=1)


def expert_kernel(own_ref, low_ref, high_ref, gate_ref, up_ref, out_ref):
    slots, units = gate_ref.shape
    total = own_ref[...] + low_ref[...] + high_ref[...]
    upward, weight = total[:, :units], total[:, units:]
    gate_pre, up_pre = gate_ref[...], up_ref[...]
    sigmoid = jax.nn.sigmoid(gate_pre)
    activated = gate_pre * sigmoid
    hidden = activated * up_pre
    part_prob = jnp.sum(hidden * upward, axis=1, keepdims=True)
    hidden_grad = weight * upward
    gate_grad = hidden_grad * up_pre * sigmoid * (1.0 + gate_pre * (1.0 - sigmoid))
    up_grad = hidden_grad * activated
    lane = lax.broadcasted_iota(jnp.int32, (slots, units), 1)
    high = part_prob.astype(BF16).astype(F32)
    prob = jnp.where(lane == 0, high, part_prob - high)
    both = jnp.concatenate([gate_grad, up_grad], axis=1)
    rest = jnp.concatenate([hidden * weight, prob], axis=1)
    out_ref[...] = jnp.concatenate([both, rest], axis=1).astype(BF16)


def back_kernel(part_ref, own_ref, low_ref, high_ref, own_w_ref, low_w_ref, high_w_ref, out_ref):
    experts, cap, width = out_ref.shape
    slots, units = own_ref.shape[0], own_ref.shape[1] // 4
    pairs = ((own_ref, own_w_ref), (low_ref, low_w_ref), (high_ref, high_w_ref))
    left = jnp.concatenate([ref[:, : 2 * units] for ref, _ in pairs], axis=1)
    right = jnp.concatenate([ref[: 2 * units] for _, ref in pairs], axis=0)
    grads = jnp.dot(left, right, preferred_element_type=F32)
    prob = jnp.zeros((slots, 1), F32)
    for ref, _ in pairs:
        prob = prob + jnp.sum(
            ref[:, 2 * units :].astype(F32)[:, units : units + 2], axis=1, keepdims=True
        )
    high = prob.astype(BF16).astype(F32)
    lane = lax.broadcasted_iota(jnp.int32, (slots, LANES), 1)
    prob = jnp.where(lane == 0, high, prob - high)
    last = jnp.where(part_ref[0] == PARTS - 1, prob, grads[:, width - LANES :])
    grads = jnp.concatenate([grads[:, : width - LANES], last], axis=1)
    out_ref[...] = grads.reshape(experts, cap, width).astype(BF16)


def down_kernel(rows_ref, own_ref, low_ref, high_ref, own_out_ref, low_out_ref, high_out_ref):
    units = own_ref.shape[1] // 4
    tn = (((0,), (0,)), ((), ()))
    left = jnp.concatenate(
        [ref[:, 2 * units : 3 * units] for ref in (own_ref, low_ref, high_ref)], axis=1
    )
    grads = lax.dot_general(left, rows_ref[...], tn, preferred_element_type=F32).astype(BF16)
    for at, ref in enumerate((own_out_ref, low_out_ref, high_out_ref)):
        ref[...] = grads[at * units : (at + 1) * units]


def join_kernel(part_ref, own_ref, low_ref, high_ref, out_ref, stage_ref):
    units, width = own_ref.shape
    part = part_ref[0]
    above, below = lax.rem(part + 1, PARTS), lax.rem(part + PARTS - 1, PARTS)
    for ref, place in ((own_ref, part), (low_ref, below), (high_ref, above)):
        stage_ref[:, pl.ds(pl.multiple_of(place * width, LANES), width)] = ref[...]
    out_ref[...] = stage_ref[:, : out_ref.shape[1]]


def combine_kernel(cap, part_ref, back_ref, ids_ref, got_ref, out_ref):
    peers, own, width = out_ref.shape
    tokens = peers * own
    experts, _, _ = got_ref.shape
    slots = experts * cap
    got = got_ref[...].astype(F32).reshape(slots, width)
    back = back_ref[...]
    sums = jnp.dot(back, got.astype(BF16), preferred_element_type=F32)[:tokens]
    turned = got[:, width - LANES :].T
    prob = turned[:1, :] + turned[1:2, :]
    picked = back[:tokens].astype(F32) * prob
    expert = lax.broadcasted_iota(jnp.int32, (tokens, slots), 1) // cap
    ids = ids_ref[...]
    lane = lax.broadcasted_iota(jnp.int32, (tokens, LANES), 1)
    by_choice = jnp.zeros((tokens, LANES), F32)
    for k in range(ids.shape[1]):
        one = jnp.sum(
            jnp.where(expert == ids[:, k : k + 1], picked, 0.0), axis=1, keepdims=True
        )
        high = one.astype(BF16).astype(F32)
        by_choice = jnp.where(lane == k, high, by_choice)
        by_choice = jnp.where(lane == k + ids.shape[1], one - high, by_choice)
    last = jnp.where(part_ref[0] == PARTS - 1, by_choice, sums[:, width - LANES :])
    sums = jnp.concatenate([sums[:, : width - LANES], last], axis=1)
    out_ref[...] = sums.reshape(peers, own, width).astype(BF16)


def finish_kernel(got_ref, tokens_ref, probs_ref):
    peers, _, width = got_ref.shape
    model = tokens_ref.shape[1]
    for part in range(PARTS):
        total = got_ref[part].astype(F32)
        for peer in range(part + PARTS, peers, PARTS):
            total = total + got_ref[peer].astype(F32)
        low = part * width
        high = min(low + width, model)
        tokens_ref[:, low:high] = total[:, : high - low].astype(BF16)
        if part == PARTS - 1:
            top = probs_ref.shape[1]
            last = total[:, width - LANES :]
            probs_ref[...] = last[:, :top] + last[:, top : 2 * top]


def body(grad_out, probs, expert_ids, saved_inputs, w_gate, w_up, w_down):
    tp_count = lax.axis_size("tp")
    experts, cap, model = saved_inputs.shape[1:]
    slots = experts * cap
    own, top = grad_out.shape[1], expert_ids.shape[2]
    tokens = tp_count * own
    width = -(-(model + LANES) // (PARTS * LANES)) * LANES
    units = w_down.shape[1]
    wide = tokens + 8
    part = lax.rem(lax.axis_index("tp"), PARTS).astype(jnp.int32).reshape(1)

    def shape(*dims, dtype=BF16):
        return jax.ShapeDtypeStruct(dims, dtype)

    def trade(to_low, to_high):
        rise = [(i, (i + 1) % tp_count) for i in range(tp_count)]
        fall = [(i, (i - 1) % tp_count) for i in range(tp_count)]
        return lax.ppermute(to_high, "tp", rise), lax.ppermute(to_low, "tp", fall)

    thirds = call(thirds_kernel, shape(tp_count, own, width), [VMEM], 0, 100000)(grad_out[0])
    thirds, gate_rows, up_rows, down_rows = lax.optimization_barrier(
        (thirds, w_gate[0].T, w_up[0].T, w_down[0])
    )
    column = lax.all_to_all(thirds, "tp", split_axis=0, concat_axis=0, tiled=True)
    ids = expert_ids[0]
    pick, back = call(
        lambda *refs: route_kernel(cap, *refs),
        [shape(slots, wide), shape(wide, slots)],
        [VMEM] * 2,
        1000000,
        100000,
    )(ids.T, probs[0].T)
    slab = shape(3 * units, width)
    own_w, to_high_w, to_low_w = call(
        weights_kernel,
        [slab, slab, slab],
        [SMEM] + [VMEM] * 3,
        0,
        12 * units * model,
        (pltpu.VMEM((3 * units, PARTS * width), BF16),),
    )(part, gate_rows, up_rows, down_rows)
    low_w, high_w = trade(to_low_w, to_high_w)
    sent = call(
        send_kernel,
        shape(experts, cap, width),
        [SMEM, VMEM, VMEM],
        2 * slots * wide * width,
        2 * slots * width,
    )(part, pick, column)
    mine = lax.all_to_all(sent, COLUMN, split_axis=0, concat_axis=0, tiled=True)

    rows_input = saved_inputs[0].reshape(slots, model)
    gate_pre = jnp.dot(rows_input, w_gate[0], preferred_element_type=F32)
    up_pre = jnp.dot(rows_input, w_up[0], preferred_element_type=F32)
    mine, gate_pre, up_pre = lax.optimization_barrier((mine, gate_pre, up_pre))
    wide_sum = shape(slots, 2 * units, dtype=F32)
    rows, up_own, up_to_low, up_to_high = call(
        upward_kernel,
        [shape(slots, width), wide_sum, wide_sum, wide_sum],
        [SMEM] + [VMEM] * 4,
        6 * slots * width * units,
        4 * slots * width,
    )(part, mine, own_w, low_w, high_w)
    up_low, up_high = trade(up_to_low, up_to_high)
    terms = call(
        expert_kernel, shape(slots, 4 * units), [VMEM] * 5, 20 * slots * units, 20 * slots * units
    )(up_own, up_low, up_high, gate_pre, up_pre)
    low_terms, high_terms = trade(terms, terms)
    summed = call(
        back_kernel,
        shape(experts, cap, width),
        [SMEM] + [VMEM] * 6,
        12 * slots * width * units,
        2 * slots * width,
    )(part, terms, low_terms, high_terms, own_w, low_w, high_w)
    summed, terms, low_terms, high_terms = lax.optimization_barrier(
        (summed, terms, low_terms, high_terms)
    )
    got = lax.all_to_all(summed, COLUMN, split_axis=0, concat_axis=0, tiled=True)

    tn = (((0,), (0,)), ((), ()))
    strip = shape(units, width)
    down_own, down_to_low, down_to_high = call(
        down_kernel, [strip] * 3, [VMEM] * 4, 6 * slots * units * width, 2 * slots * width
    )(rows, terms, low_terms, high_terms)
    down_low, down_high = trade(down_to_low, down_to_high)
    grad_gate = lax.dot_general(
        rows_input, terms[:, :units], tn, preferred_element_type=F32
    )
    grad_up = lax.dot_general(
        rows_input, terms[:, units : 2 * units], tn, preferred_element_type=F32
    )
    grad_down = call(
        join_kernel,
        shape(units, model),
        [SMEM] + [VMEM] * 3,
        0,
        4 * units * model,
        (pltpu.VMEM((units, PARTS * width), BF16),),
    )(part, down_own, down_low, down_high)

    combined = call(
        lambda *refs: combine_kernel(cap, *refs),
        shape(tp_count, own, width),
        [SMEM] + [VMEM] * 3,
        2 * slots * wide * width,
        2 * slots * width,
    )(part, back, ids, got)
    last = lax.all_to_all(combined, "tp", split_axis=0, concat_axis=0, tiled=True)
    grad_tokens, grad_probs = call(
        finish_kernel,
        [shape(own, model), shape(own, top, dtype=F32)],
        [VMEM],
        1000,
        2 * tokens * width,
    )(last)
    return (
        grad_tokens[None],
        grad_probs[None],
        grad_gate.astype(BF16)[None],
        grad_up.astype(BF16)[None],
        grad_down[None],
    )


def solution(mesh):
    placed = (
        P(COLUMN, "tp", None),
        P(COLUMN, None, None),
        P(COLUMN, None, None),
        P(COLUMN, None, None, None),
        P(COLUMN, None, "tp"),
        P(COLUMN, None, "tp"),
        P(COLUMN, "tp", None),
    )
    return jax.shard_map(
        body,
        mesh=mesh,
        in_specs=placed,
        out_specs=(
            P(COLUMN, "tp", None),
            P(COLUMN, "tp", None),
            P(COLUMN, None, "tp"),
            P(COLUMN, None, "tp"),
            P(COLUMN, "tp", None),
        ),
        check_vma=False,
    )
```

```python
import jax
import jax.numpy as jnp
from jax import lax
from jax.experimental import pallas as pl
from jax.experimental.pallas import tpu as pltpu
from jax.sharding import PartitionSpec as P

PARTS = 3
LANES = 128
WEIGHT_ROWS = 16
F32, BF16 = jnp.float32, jnp.bfloat16
COLUMN = ("dp", "ctx")
VMEM = pl.BlockSpec(memory_space=pltpu.VMEM)
NT = (((1,), (1,)), ((), ()))
TN = (((0,), (0,)), ((), ()))
SMEM = pl.BlockSpec(memory_space=pltpu.SMEM)


def call(kernel, outs, in_specs, flops, bytes_accessed, scratch=()):
    return pl.pallas_call(
        kernel,
        out_shape=outs,
        in_specs=in_specs,
        out_specs=jax.tree.map(lambda _: VMEM, outs),
        scratch_shapes=scratch,
        compiler_params=pltpu.CompilerParams(vmem_limit_bytes=16 << 20),
        cost_estimate=pl.CostEstimate(
            flops=flops, bytes_accessed=bytes_accessed, transcendentals=0
        ),
    )


def route_kernel(cap, ids_ref, probs_ref, pick_ref, back_ref):
    top, tokens = ids_ref.shape
    slots, width = pick_ref.shape
    row = lax.broadcasted_iota(jnp.int32, (slots, tokens), 0)
    expert, place = row // cap, row % cap
    ids = ids_ref[...]
    probs = probs_ref[...].astype(F32)
    member = jnp.zeros((slots, tokens), F32)
    weight = jnp.zeros((slots, tokens), F32)
    for k in range(top):
        same = expert == ids[k : k + 1, :]
        member = jnp.where(same, 1.0, member)
        weight = jnp.where(same, probs[k : k + 1, :], weight)
    before = lax.broadcasted_iota(jnp.int32, (tokens, tokens), 0) < lax.broadcasted_iota(
        jnp.int32, (tokens, tokens), 1
    )
    rank = jnp.dot(
        member.astype(BF16), before.astype(F32).astype(BF16), preferred_element_type=F32
    )
    pick = jnp.where(rank == place.astype(F32), member, 0.0)
    slot_weight = jnp.sum(pick * weight, axis=1, keepdims=True)
    tail = lax.broadcasted_iota(jnp.int32, (slots, width - tokens), 1)
    full = jnp.concatenate([pick, jnp.where(tail == 0, slot_weight, 0.0)], axis=1)
    pick_ref[...] = full.astype(BF16)
    back_ref[...] = full.T.astype(BF16)


def thirds_kernel(grad_ref, out_ref):
    peers, _, width = out_ref.shape
    model = grad_ref.shape[1]
    for part in range(PARTS):
        piece = grad_ref[:, part * width : min(part * width + width, model)]
        if piece.shape[1] < width:
            piece = jnp.concatenate(
                [piece, jnp.zeros((piece.shape[0], width - piece.shape[1]), BF16)], axis=1
            )
        for peer in range(part, peers, PARTS):
            out_ref[peer] = piece


def neighbours(part):
    return lax.rem(part + 1, PARTS), lax.rem(part + PARTS - 1, PARTS)


def strip(place, width):
    return pl.ds(pl.multiple_of(place * width, LANES), width)


def weights_kernel(
    part_ref, gate_ref, up_ref, down_ref,
    own_ref, high_ref, low_ref, own_down_ref, high_down_ref, low_down_ref, stage_ref,
):
    units, model = gate_ref.shape
    width = own_ref.shape[1]
    part = part_ref[0]
    above, below = neighbours(part)
    for at, ref in enumerate((gate_ref, up_ref, down_ref)):
        stage_ref[at * units : (at + 1) * units, :model] = ref[...]
    stage_ref[:, model:] = jnp.zeros((3 * units, PARTS * width - model), BF16)
    for ref, down_out_ref, place in (
        (own_ref, own_down_ref, part),
        (high_ref, high_down_ref, above),
        (low_ref, low_down_ref, below),
    ):
        ref[...] = stage_ref[: 2 * units, strip(place, width)]
        down_out_ref[...] = stage_ref[2 * units :, strip(place, width)]


def factors_kernel(gate_ref, up_ref, out_ref):
    gate_pre, up_pre = gate_ref[...], up_ref[...]
    sigmoid = jax.nn.sigmoid(gate_pre)
    activated = gate_pre * sigmoid
    out_ref[...] = jnp.concatenate(
        [
            up_pre * sigmoid * (1.0 + gate_pre * (1.0 - sigmoid)),
            activated,
            activated * up_pre,
        ],
        axis=0,
    )


def send_kernel(part_ref, pick_ref, column_ref, out_ref):
    peers, own, width = column_ref.shape
    tokens = peers * own
    experts, cap, _ = out_ref.shape
    column = column_ref[...].astype(F32).reshape(tokens, width)
    rest = pick_ref.shape[1] - tokens
    lane = lax.broadcasted_iota(jnp.int32, (rest, width), 1)
    deep = lax.broadcasted_iota(jnp.int32, (rest, width), 0)
    padded = (deep == 0) & (lane >= width - LANES) & (part_ref[0] == PARTS - 1)
    column = jnp.concatenate([column, padded.astype(F32)], axis=0).astype(BF16)
    rows = jnp.dot(pick_ref[...], column, preferred_element_type=F32)
    out_ref[...] = rows.reshape(experts, cap, width).astype(BF16)


def upward_kernel(part_ref, got_ref, own_ref, low_ref, high_ref, factors_ref, rows_ref, out_ref):
    experts, cap, width = got_ref.shape
    slots, units = experts * cap, own_ref.shape[0]
    rows = got_ref[...].reshape(slots, width)
    rows_ref[...] = rows
    part = part_ref[0]
    above, below = neighbours(part)
    for ref, place in ((own_ref, part), (low_ref, below), (high_ref, above)):
        product = lax.dot_general(ref[...], rows, NT, preferred_element_type=F32)
        out_ref[pl.ds(pl.multiple_of(place * units, units), units)] = product.astype(BF16)
    weight = rows[:, width - LANES :].astype(F32).T[:WEIGHT_ROWS]
    low = 3 * units + WEIGHT_ROWS
    out_ref[3 * units : low] = jnp.where(part == PARTS - 1, weight, 0.0).astype(BF16)
    out_ref[low:] = factors_ref[...].astype(BF16)


def expert_kernel(
    part_ref, all_ref, own_ref, own_w_ref, low_w_ref, high_w_ref,
    out_ref, terms_ref, hidden_ref, total_ref,
):
    experts, cap, width = out_ref.shape
    slots = experts * cap
    units = own_ref.shape[0] // 3
    part = part_ref[0]
    above, below = neighbours(part)
    first = total_ref.shape[0]
    total = all_ref[0, :first].astype(F32)
    for peer in range(1, PARTS):
        total = total + all_ref[peer, :first].astype(F32)
    total_ref[...] = total
    weight = total[3 * units : 3 * units + 1]
    prob = jnp.zeros((1, slots), F32)
    left, scaled = [], []
    right = [own_w_ref[...], low_w_ref[...], high_w_ref[...]]
    for place in (part, below, above):
        upward = total_ref[pl.ds(pl.multiple_of(place * units, units), units)]
        if place is part:
            factors = own_ref[...]
        else:
            factors = all_ref[place, first:].astype(F32)
        by_gate, by_up, hidden = (factors[at * units : (at + 1) * units] for at in range(3))
        prob = prob + jnp.sum(hidden * upward, axis=0, keepdims=True)
        hidden_grad = weight * upward
        left += [hidden_grad * by_gate, hidden_grad * by_up]
        scaled.append(hidden * weight)
    left = jnp.concatenate(left, axis=0).astype(BF16)
    terms_ref[...] = left[: 2 * units]
    hidden_ref[...] = jnp.concatenate(scaled, axis=0).astype(BF16)
    grads = lax.dot_general(left, jnp.concatenate(right, axis=0), TN, preferred_element_type=F32)
    lane = lax.broadcasted_iota(jnp.int32, (LANES, slots), 0)
    high = prob.astype(BF16).astype(F32)
    prob = jnp.where(lane == 0, high, jnp.where(lane == 1, prob - high, 0.0)).T
    last = jnp.where(part == PARTS - 1, prob, grads[:, width - LANES :])
    grads = jnp.concatenate([grads[:, : width - LANES], last], axis=1)
    out_ref[...] = grads.reshape(experts, cap, width).astype(BF16)


def down_kernel(rows_ref, hidden_ref, own_out_ref, low_out_ref, high_out_ref):
    units = own_out_ref.shape[0]
    grads = jnp.dot(hidden_ref[...], rows_ref[...], preferred_element_type=F32).astype(BF16)
    for at, ref in enumerate((own_out_ref, low_out_ref, high_out_ref)):
        ref[...] = grads[at * units : (at + 1) * units]


def join_kernel(part_ref, own_ref, low_ref, high_ref, out_ref, stage_ref):
    units, width = own_ref.shape
    part = part_ref[0]
    above, below = neighbours(part)
    for ref, place in ((own_ref, part), (low_ref, below), (high_ref, above)):
        stage_ref[:, strip(place, width)] = ref[...]
    out_ref[...] = stage_ref[:, : out_ref.shape[1]]


def combine_kernel(cap, part_ref, back_ref, ids_ref, got_ref, out_ref):
    peers, own, width = out_ref.shape
    tokens = peers * own
    experts, _, _ = got_ref.shape
    slots = experts * cap
    got = got_ref[...].astype(F32).reshape(slots, width)
    back = back_ref[...]
    sums = jnp.dot(back, got.astype(BF16), preferred_element_type=F32)[:tokens]
    turned = got[:, width - LANES :].T
    prob = turned[:1, :] + turned[1:2, :]
    picked = back[:tokens].astype(F32) * prob
    expert = lax.broadcasted_iota(jnp.int32, (tokens, slots), 1) // cap
    ids = ids_ref[...]
    lane = lax.broadcasted_iota(jnp.int32, (tokens, LANES), 1)
    by_choice = jnp.zeros((tokens, LANES), F32)
    for k in range(ids.shape[1]):
        one = jnp.sum(
            jnp.where(expert == ids[:, k : k + 1], picked, 0.0), axis=1, keepdims=True
        )
        high = one.astype(BF16).astype(F32)
        by_choice = jnp.where(lane == k, high, by_choice)
        by_choice = jnp.where(lane == k + ids.shape[1], one - high, by_choice)
    last = jnp.where(part_ref[0] == PARTS - 1, by_choice, sums[:, width - LANES :])
    sums = jnp.concatenate([sums[:, : width - LANES], last], axis=1)
    out_ref[...] = sums.reshape(peers, own, width).astype(BF16)


def finish_kernel(got_ref, tokens_ref, probs_ref):
    peers, _, width = got_ref.shape
    model = tokens_ref.shape[1]
    for part in range(PARTS):
        total = got_ref[part].astype(F32)
        for peer in range(part + PARTS, peers, PARTS):
            total = total + got_ref[peer].astype(F32)
        low = part * width
        high = min(low + width, model)
        tokens_ref[:, low:high] = total[:, : high - low].astype(BF16)
        if part == PARTS - 1:
            top = probs_ref.shape[1]
            last = total[:, width - LANES :]
            probs_ref[...] = last[:, :top] + last[:, top : 2 * top]


def body(grad_out, probs, expert_ids, saved_inputs, w_gate, w_up, w_down):
    tp_count = lax.axis_size("tp")
    experts, cap, model = saved_inputs.shape[1:]
    slots = experts * cap
    own, top = grad_out.shape[1], expert_ids.shape[2]
    tokens = tp_count * own
    width = -(-(model + LANES) // (PARTS * LANES)) * LANES
    units = w_down.shape[1]
    wide = tokens + 8
    part = lax.rem(lax.axis_index("tp"), PARTS).astype(jnp.int32).reshape(1)

    def shape(*dims, dtype=BF16):
        return jax.ShapeDtypeStruct(dims, dtype)

    groups = [list(range(at, at + PARTS)) for at in range(0, tp_count, PARTS)]

    def trade(to_low, to_high):
        rise = [(g[i], g[(i + 1) % PARTS]) for g in groups for i in range(PARTS)]
        fall = [(g[(i + 1) % PARTS], g[i]) for g in groups for i in range(PARTS)]
        return lax.ppermute(to_high, "tp", rise), lax.ppermute(to_low, "tp", fall)

    thirds = call(thirds_kernel, shape(tp_count, own, width), [VMEM], 0, 100000)(grad_out[0])
    thirds, gate_rows, up_rows, down_rows = lax.optimization_barrier(
        (thirds, w_gate[0].T, w_up[0].T, w_down[0])
    )
    column = lax.all_to_all(thirds, "tp", split_axis=0, concat_axis=0, tiled=True)
    ids = expert_ids[0]
    pick, back = call(
        lambda *refs: route_kernel(cap, *refs),
        [shape(slots, wide), shape(wide, slots)],
        [VMEM] * 2,
        1000000,
        100000,
    )(ids.T, probs[0].T)
    slab, thin = shape(2 * units, width), shape(units, width)
    own_w, high_w, low_w, own_down, high_down, low_down = call(
        weights_kernel,
        [slab] * 3 + [thin] * 3,
        [SMEM] + [VMEM] * 3,
        0,
        12 * units * model,
        (pltpu.VMEM((3 * units, PARTS * width), BF16),),
    )(part, gate_rows, up_rows, down_rows)
    pick, high_w, low_w, high_down, low_down = lax.optimization_barrier(
        (pick, high_w, low_w, high_down, low_down)
    )
    from_low_down, from_high_down = trade(low_down, high_down)
    from_low_w, from_high_w = trade(low_w, high_w)
    sent = call(
        send_kernel,
        shape(experts, cap, width),
        [SMEM, VMEM, VMEM],
        2 * slots * wide * width,
        2 * slots * width,
    )(part, pick, column)
    mine = lax.all_to_all(sent, COLUMN, split_axis=0, concat_axis=0, tiled=True)

    rows_input = saved_inputs[0].reshape(slots, model)
    gate_pre = lax.dot_general(gate_rows, rows_input, NT, preferred_element_type=F32)
    up_pre = lax.dot_general(up_rows, rows_input, NT, preferred_element_type=F32)
    factors = call(
        factors_kernel,
        shape(3 * units, slots, dtype=F32),
        [VMEM] * 2,
        20 * slots * units,
        20 * slots * units,
    )(gate_pre, up_pre)
    rows, partial = call(
        upward_kernel,
        [shape(slots, width), shape(6 * units + WEIGHT_ROWS, slots)],
        [SMEM] + [VMEM] * 5,
        6 * slots * width * units,
        4 * slots * width,
    )(part, mine, own_down, from_low_down, from_high_down, factors)
    partials = lax.all_gather(partial, "tp", axis=0, axis_index_groups=groups)
    summed, terms, hidden = call(
        expert_kernel,
        [shape(experts, cap, width), shape(2 * units, slots), shape(3 * units, slots)],
        [SMEM] + [VMEM] * 5,
        12 * slots * width * units,
        2 * slots * width,
        (pltpu.VMEM((3 * units + WEIGHT_ROWS, slots), F32),),
    )(part, partials, factors, own_w, from_low_w, from_high_w)
    summed, terms, hidden = lax.optimization_barrier((summed, terms, hidden))
    got = lax.all_to_all(summed, COLUMN, split_axis=0, concat_axis=0, tiled=True)

    down_own, down_to_low, down_to_high = call(
        down_kernel, [thin] * 3, [VMEM] * 2, 6 * slots * units * width, 2 * slots * width
    )(rows, hidden)
    down_low, down_high = trade(down_to_low, down_to_high)
    grad_gate = jnp.dot(terms[:units], rows_input, preferred_element_type=F32).astype(BF16)
    grad_up = jnp.dot(terms[units:], rows_input, preferred_element_type=F32).astype(BF16)
    got, grad_gate, down_own = lax.optimization_barrier((got, grad_gate, down_own))
    grad_down = call(
        join_kernel,
        shape(units, model),
        [SMEM] + [VMEM] * 3,
        0,
        4 * units * model,
        (pltpu.VMEM((units, PARTS * width), BF16),),
    )(part, down_own, down_low, down_high)
    combined = call(
        lambda *refs: combine_kernel(cap, *refs),
        shape(tp_count, own, width),
        [SMEM] + [VMEM] * 3,
        2 * slots * wide * width,
        2 * slots * width,
    )(part, back, ids, got)
    last = lax.all_to_all(combined, "tp", split_axis=0, concat_axis=0, tiled=True)
    grad_tokens, grad_probs = call(
        finish_kernel,
        [shape(own, model), shape(own, top, dtype=F32)],
        [VMEM],
        1000,
        2 * tokens * width,
    )(last)
    return (
        grad_tokens[None],
        grad_probs[None],
        grad_gate.T[None],
        grad_up.T[None],
        grad_down[None],
    )


def solution(mesh):
    placed = (
        P(COLUMN, "tp", None),
        P(COLUMN, None, None),
        P(COLUMN, None, None),
        P(COLUMN, None, None, None),
        P(COLUMN, None, "tp"),
        P(COLUMN, None, "tp"),
        P(COLUMN, "tp", None),
    )
    return jax.shard_map(
        body,
        mesh=mesh,
        in_specs=placed,
        out_specs=(
            P(COLUMN, "tp", None),
            P(COLUMN, "tp", None),
            P(COLUMN, None, "tp"),
            P(COLUMN, None, "tp"),
            P(COLUMN, "tp", None),
        ),
        check_vma=False,
    )
```
